32 devices in a mesh: mod: 2 (over x), loop: 4 (over z), line: 4 (over y, core).
Axes of the slice: x: 2, y: 2, z: 4, core: 2. Of those that a mesh axis runs over, the one named last changes fastest.
Arguments:
- act: bfloat16 [2, 12288, 512], P('mod', ('loop', 'line'))
- dy: bfloat16 [2, 12288, 1280], P('mod', ('loop', 'line')), may hold values from -6 to 6
- w_out: bfloat16 [2, 512, 1280], P('mod'), may hold values from -0.15625 to 0.15625
- counts: int32 [2, 4, 4], P('mod', 'loop', 'line'), may hold values from 192 to 768, as said below
Outputs:
- grad_clipped: float32 [2, 512, 1280], P('mod', 'loop')
- hidden_grad: bfloat16 [2, 12288, 512], P('mod', ('loop', 'line'))
The draws below stay inside these ranges and needn't reach their ends.
Inputs may be any that keep to these rules, and one draw needn't show every extreme that they name: `counts`: in each tower some device has all 768 slots live.
All inputs are finite; a program needn't handle non-finite values.
Results may differ from the reference program's by a relative error of at most 0.001.
Values sent between devices are 32-bit elements; how exact they have to be, the bound alone decides.
No kernel may reach another device: no remote copies, remote signals or barrier semaphores. Data moves between devices by JAX's collectives and lax.ppermute only.
A program may use at most 64 MiB of HBM per device.

```python
import jax
import jax.numpy as jnp
from jax import lax

H = 512
DB = 1280
ROWS = 768
TOTAL = 12288
N_MOD = 2
N_LOOP = 4
N_LINE = 4


def draw_act(key, part):
    total_rows = ROWS * N_LOOP * N_LINE
    first, second, third = jax.random.split(key, 3)
    place = (lax.broadcasted_iota(jnp.float32, (N_MOD, 1, H), 0) * H + lax.broadcasted_iota(jnp.float32, (N_MOD, 1, H), 2)) / (N_MOD * H)
    column_scale = jnp.exp(place * jnp.log(3.0)) * jnp.exp(jax.random.uniform(second, (N_MOD, 1, H), jnp.float32, 0.0, 1.15))
    row_scale = jnp.exp(jax.random.uniform(third, (N_MOD, total_rows, 1), jnp.float32, 0.0, 1.15))
    base = jax.random.normal(first, (N_MOD, total_rows, H), jnp.float32)
    return jnp.clip(base * row_scale * column_scale * 0.35, -8.0, 8.0).astype(jnp.bfloat16)


def draw_counts(key, part):
    first, second = jax.random.split(jax.random.fold_in(key, 11))
    values = jax.random.randint(first, (N_MOD, N_LOOP, N_LINE), ROWS // 4, ROWS + 1)
    chosen = jax.random.randint(second, (N_MOD, 1, 1), 0, N_LOOP * N_LINE)
    device = lax.broadcasted_iota(jnp.int32, (N_MOD, N_LOOP, N_LINE), 1) * N_LINE + lax.broadcasted_iota(jnp.int32, (N_MOD, N_LOOP, N_LINE), 2)
    return jnp.where(device == chosen, ROWS, values).astype(jnp.int32)


def shard_levels(stream_key, dims, shards, least, largest):
    gain, own = 1.0, jax.random.fold_in(stream_key, 6)
    for position, blocks in shards:
        heights = jnp.exp(jax.random.uniform(jax.random.fold_in(own, position), (blocks,), jnp.float32, least / len(shards), largest / len(shards)))
        gain = gain * jnp.repeat(heights, dims[position] // blocks).reshape([-1 if axis == position else 1 for axis in range(len(dims))])
    return gain


def scatter_about(key, dims, spread, most, cuts=(), kind=jnp.bfloat16):
    entries = jax.random.normal(key, dims, jnp.float32) * spread
    if len(cuts) > 0:
        entries = shard_levels(key, dims, cuts, -0.22, 0.18) * entries
    return jnp.clip(entries, min=-most, max=most).astype(kind)


def setup_inputs(seed: int = 0) -> dict:
    key_list = jax.random.split(jax.random.key(seed), 5)
    act = draw_act(jax.random.fold_in(key_list[4], 71), 0)
    dy = scatter_about(key_list[1], (N_MOD, TOTAL, DB), 1.0, 6.0, ((0, 2), (1, 16)))
    w_out = scatter_about(key_list[2], (N_MOD, H, DB), DB ** -0.5, 0.15625, ((0, 2),))
    counts = draw_counts(jax.random.fold_in(key_list[4], 71), 0)
    return {"act": act, "dy": dy, "w_out": w_out, "counts": counts}


def reference(act, dy, w_out, counts):
    flat = counts.reshape(N_MOD, N_LOOP * N_LINE)
    limit = jnp.repeat(flat, ROWS, axis=1)
    within = (jnp.arange(ROWS * N_LOOP * N_LINE, dtype=jnp.int32) % ROWS)[None, :]
    live = (within < limit)[:, :, None]
    masked = jnp.where(live, act, jnp.zeros_like(act))
    grads = []
    hiddens = []
    for tower in range(N_MOD):
        grads.append(lax.dot_general(masked[tower], dy[tower], (((0,), (0,)), ((), ())), preferred_element_type=jnp.float32))
        back = lax.dot_general(dy[tower], w_out[tower], (((1,), (1,)), ((), ())), preferred_element_type=jnp.float32)
        hiddens.append(jnp.where(live[tower], back, jnp.zeros_like(back)).astype(jnp.bfloat16))
    grad = jnp.stack(grads)
    total = jnp.sum(grad * grad)
    factor = 1.0 / jnp.sqrt(total / (N_MOD * H * DB) + 1e-06)
    return (grad * factor, jnp.stack(hiddens))
```

```python
import jax
import jax.numpy as jnp
from jax import lax
from jax.sharding import PartitionSpec as P

CORES = 2


def swap(x, axis, distance):
    size = lax.axis_size(axis)
    return lax.ppermute(x, axis, [(i, i ^ distance) for i in range(size)])


def doubled(size):
    distance = 1
    while distance < size:
        yield distance
        distance *= 2


def piece(x, index):
    return lax.dynamic_index_in_dim(x, index, 0, keepdims=False)


def scatter_sum(x, axis, index, stride=1):
    size = x.shape[0]
    got = [swap(piece(x, index ^ d), axis, d * stride) for d in range(1, size)]
    total = piece(x, index)
    for part in got:
        total = total + part
    return total


def on_device(act, dy, w_out, counts):
    tokens = act[0]
    upstream = dy[0]
    weight = w_out[0]
    rows, hidden = tokens.shape
    block = weight.shape[1]
    n_loop = lax.axis_size("loop")
    n_y = lax.axis_size("line") // CORES
    z = lax.axis_index("loop")
    line = lax.axis_index("line")
    core = line % CORES
    y = line // CORES
    own_rows = hidden // n_loop
    half = block // CORES
    first = half * 3 // 5 // 128 * 128

    live = lax.broadcasted_iota(jnp.int32, (rows, 1), 0) < counts[0, 0]
    masked = jnp.where(live, tokens, jnp.zeros_like(tokens))
    entries = lax.axis_size("mod") * hidden * block

    def term(start, width):
        columns = lax.dynamic_slice_in_dim(upstream, start, width, 1)
        return lax.dot_general(
            masked, columns, (((0,), (0,)), ((), ())), preferred_element_type=jnp.float32
        )

    def chip_sum(start, width):
        other = swap(term((1 - core) * half + start, width), "line", 1)
        return term(core * half + start, width) + other

    late = chip_sum(first, half - first).reshape(n_loop, own_rows, half - first)
    early = chip_sum(0, first).reshape(n_loop, n_y, own_rows // n_y, first)
    early = scatter_sum(early.transpose(1, 0, 2, 3), "line", y, CORES)
    late = scatter_sum(late, "loop", z)
    early = scatter_sum(early, "loop", z)
    for d in doubled(n_y):
        late = late + swap(late, "line", d * CORES)

    squares = jnp.sum(early * early, axis=0).reshape(-1, 128).sum(0)
    squares_late = jnp.sum(late * late, axis=0).reshape(-1, 128).sum(0)
    total = (squares + jnp.where(y == 0, squares_late, 0.0)).reshape(1, 128)
    for d in doubled(n_y * CORES):
        total = total + swap(total, "line", d)
    for d in doubled(n_loop):
        total = total + swap(total, "loop", d)
    for d in doubled(lax.axis_size("mod")):
        total = total + swap(total, "mod", d)
    factor = 1.0 / jnp.sqrt(jnp.sum(total) / entries + 1e-06)

    early = early[None]
    for d in doubled(n_y):
        other = swap(early, "line", d * CORES)
        upper = (y // d) % 2 == 1
        early = jnp.where(
            upper, jnp.concatenate([other, early]), jnp.concatenate([early, other])
        )
    mine = jnp.concatenate([early.reshape(own_rows, first), late], axis=1)
    other = swap(mine, "line", 1)
    share = jnp.where(
        core == 1,
        jnp.concatenate([other, mine], axis=1),
        jnp.concatenate([mine, other], axis=1),
    )
    clipped = share * factor

    back = lax.dot_general(
        upstream, weight, (((1,), (1,)), ((), ())), preferred_element_type=jnp.float32
    )
    hidden_grad = jnp.where(live, back, jnp.zeros_like(back)).astype(jnp.bfloat16)
    return (clipped[None], hidden_grad[None])


def solution(mesh):
    in_specs = (
        P("mod", ("loop", "line"), None),
        P("mod", ("loop", "line"), None),
        P("mod", None, None),
        P("mod", "loop", "line"),
    )
    out_specs = (P("mod", "loop", None), P("mod", ("loop", "line"), None))
    return jax.shard_map(
        on_device, mesh=mesh, in_specs=in_specs, out_specs=out_specs, check_vma=False
    )
```

```python
import jax
import jax.numpy as jnp
from jax import lax
from jax.sharding import PartitionSpec as P

CORES = 2


def swap(x, axis, distance):
    size = lax.axis_size(axis)
    return lax.ppermute(x, axis, [(i, i ^ distance) for i in range(size)])


def doubled(size):
    distance = 1
    while distance < size:
        yield distance
        distance *= 2


def after(x, *ready):
    return lax.optimization_barrier((x, *ready))[0]


def piece(x, index):
    return lax.dynamic_index_in_dim(x, index, 0, keepdims=False)


def scatter_sum(x, axis, index, stride=1):
    size = x.shape[0]
    order = sorted(range(1, size), key=lambda d: -(d ^ 1))
    got = [swap(piece(x, index ^ d), axis, d * stride) for d in order]
    total = piece(x, index)
    for part in got:
        total = total + part
    return total


def on_device(act, dy, w_out, counts):
    tokens = act[0]
    upstream = dy[0]
    weight = w_out[0]
    rows, hidden = tokens.shape
    block = weight.shape[1]
    n_loop = lax.axis_size("loop")
    n_y = lax.axis_size("line") // CORES
    z = lax.axis_index("loop")
    line = lax.axis_index("line")
    core = line % CORES
    y = line // CORES
    own_rows = hidden // n_loop
    half = block // CORES
    first = half * 3 // 5 // 128 * 128

    live = lax.broadcasted_iota(jnp.int32, (rows, 1), 0) < counts[0, 0]
    masked = jnp.where(live, tokens, jnp.zeros_like(tokens))
    entries = lax.axis_size("mod") * hidden * block

    def term(start, width, *ready):
        columns = lax.dynamic_slice_in_dim(after(upstream, *ready), start, width, 1)
        return lax.dot_general(
            masked, columns, (((0,), (0,)), ((), ())), preferred_element_type=jnp.float32
        )

    early_other = swap(term((1 - core) * half, first), "line", 1)
    late_other = swap(term((1 - core) * half + first, half - first), "line", 1)
    early = term(core * half, first) + early_other
    late = term(core * half + first, half - first, early) + late_other
    back = lax.dot_general(
        after(upstream, late), weight, (((1,), (1,)), ((), ())), preferred_element_type=jnp.float32
    )
    hidden_grad = jnp.where(live, back, jnp.zeros_like(back)).astype(jnp.bfloat16)

    early = early.reshape(n_loop, n_y, own_rows // n_y, first).transpose(1, 0, 2, 3)
    early = scatter_sum(early, "line", y, CORES)
    late = scatter_sum(late.reshape(n_loop, own_rows, half - first), "loop", z)
    early_part = early
    early = scatter_sum(early, "loop", z)
    late = after(late, early_part)
    for d in doubled(n_y):
        late = late + swap(late, "line", d * CORES)

    squares = jnp.sum(early * early, axis=0).reshape(-1, 128).sum(0)
    squares_late = jnp.sum(late * late, axis=0).reshape(-1, 128).sum(0)
    total = (squares + jnp.where(y == 0, squares_late, 0.0)).reshape(1, 128)
    total = after(total, hidden_grad)
    for d in doubled(CORES):
        total = total + swap(total, "line", d)
    spread = total
    for d in doubled(n_loop):
        total = total + swap(total, "loop", d)
    for d in doubled(lax.axis_size("mod")):
        total = total + swap(total, "mod", d)
    over_towers = total
    for d in doubled(n_y):
        total = total + swap(total, "line", d * CORES)
    factor = 1.0 / jnp.sqrt(jnp.sum(total) / entries + 1e-06)

    early = after(early, spread)[None]
    for d in doubled(n_y):
        other = after(swap(early, "line", d * CORES), over_towers)
        upper = (y // d) % 2 == 1
        early = jnp.where(
            upper, jnp.concatenate([other, early]), jnp.concatenate([early, other])
        )
    mine = jnp.concatenate([early.reshape(own_rows, first), late], axis=1)
    other = swap(mine, "line", 1)
    share = jnp.where(
        core == 1,
        jnp.concatenate([other, mine], axis=1),
        jnp.concatenate([mine, other], axis=1),
    )
    clipped = share * factor

    return (clipped[None], hidden_grad[None])


def solution(mesh):
    in_specs = (
        P("mod", ("loop", "line"), None),
        P("mod", ("loop", "line"), None),
        P("mod", None, None),
        P("mod", "loop", "line"),
    )
    out_specs = (P("mod", "loop", None), P("mod", ("loop", "line"), None))
    return jax.shard_map(
        on_device, mesh=mesh, in_specs=in_specs, out_specs=out_specs, check_vma=False
    )
```

```python
import jax
import jax.numpy as jnp
from jax import lax
from jax.experimental import pallas as pl
from jax.experimental.pallas import tpu as pltpu
from jax.sharding import PartitionSpec as P

CORES = 2
VMEM_BYTES = 12 * 2**20


def swap(x, axis, distance):
    size = lax.axis_size(axis)
    return lax.ppermute(x, axis, [(i, i ^ distance) for i in range(size)])


def doubled(size):
    distance = 1
    while distance < size:
        yield distance
        distance *= 2


def after(x, *ready):
    return lax.optimization_barrier((x, *ready))[0]


def piece(x, index):
    return lax.dynamic_index_in_dim(x, index, 0, keepdims=False)


def scatter_sum(x, axis, index, stride=1):
    size = x.shape[0]
    order = sorted(range(1, size), key=lambda d: -(d ^ 1))
    got = [swap(piece(x, index[d]), axis, d * stride) for d in order]
    total = piece(x, index[0])
    for part in got:
        total = total + part
    return total


def product(left, right):
    return lax.dot_general(
        left, right, (((0,), (0,)), ((), ())), preferred_element_type=jnp.float32
    )


def first_kernel(count, core, act, dy, out, masked, late, own, tokens, early, sems):
    half = own.shape[1]
    first = early.shape[1]
    other = pl.multiple_of((1 - core[0]) * half, 128)
    mine = pl.multiple_of(core[0] * half, 128)
    copies = [
        pltpu.make_async_copy(act, tokens, sems.at[0]),
        pltpu.make_async_copy(dy.at[:, pl.ds(other, first)], early, sems.at[1]),
        pltpu.make_async_copy(dy.at[:, pl.ds(other + first, half - first)], late, sems.at[2]),
        pltpu.make_async_copy(dy.at[:, pl.ds(mine, half)], own, sems.at[3]),
    ]
    for copy in copies:
        copy.start()
    copies[0].wait()
    live = lax.broadcasted_iota(jnp.int32, (act.shape[0], 1), 0) < count[0, 0, 0]
    masked[...] = jnp.where(live, tokens[...], jnp.zeros_like(tokens))
    copies[1].wait()
    out[...] = product(masked[...], early[...])
    copies[2].wait()
    copies[3].wait()


def first_term(counts, core, act, dy, half, first):
    rows, hidden = act.shape
    smem = pl.BlockSpec(memory_space=pltpu.SMEM)
    vmem = pl.BlockSpec(memory_space=pltpu.VMEM)
    hbm = pl.BlockSpec(memory_space=pltpu.HBM)
    return pl.pallas_call(
        first_kernel,
        out_shape=(
            jax.ShapeDtypeStruct((hidden, first), jnp.float32),
            jax.ShapeDtypeStruct((rows, hidden), act.dtype),
            jax.ShapeDtypeStruct((rows, half - first), dy.dtype),
            jax.ShapeDtypeStruct((rows, half), dy.dtype),
        ),
        in_specs=[smem, smem, hbm, hbm],
        out_specs=(vmem,) * 4,
        scratch_shapes=[
            pltpu.VMEM((rows, hidden), act.dtype),
            pltpu.VMEM((rows, first), dy.dtype),
            pltpu.SemaphoreType.DMA((4,)),
        ],
        compiler_params=pltpu.CompilerParams(vmem_limit_bytes=VMEM_BYTES),
    )(
        counts,
        core,
        pltpu.with_memory_space_constraint(act, pltpu.HBM),
        pltpu.with_memory_space_constraint(dy, pltpu.HBM),
    )


def terms_kernel(masked, columns, *outs):
    start = 0
    for out in outs:
        width = out.shape[1]
        out[...] = product(masked[...], columns[:, start : start + width])
        start += width


def terms(masked, columns, *widths):
    vmem = pl.BlockSpec(memory_space=pltpu.VMEM)
    hidden = masked.shape[1]
    return pl.pallas_call(
        terms_kernel,
        out_shape=tuple(jax.ShapeDtypeStruct((hidden, w), jnp.float32) for w in widths),
        in_specs=[vmem, vmem],
        out_specs=(vmem,) * len(widths),
        compiler_params=pltpu.CompilerParams(vmem_limit_bytes=VMEM_BYTES),
    )(masked, columns)


def on_device(act, dy, w_out, counts):
    tokens = act[0]
    upstream = dy[0]
    weight = w_out[0]
    rows, hidden = tokens.shape
    block = weight.shape[1]
    n_loop = lax.axis_size("loop")
    n_y = lax.axis_size("line") // CORES
    z = lax.axis_index("loop").astype(jnp.uint32)
    line = lax.axis_index("line").astype(jnp.uint32)
    y = line // CORES
    core, low_core, low_y, over_z, over_y, upper = lax.optimization_barrier(
        (
            (line % CORES).astype(jnp.int32).reshape(1),
            line % CORES == 0,
            y == 0,
            [z ^ d for d in range(n_loop)],
            [y ^ d for d in range(n_y)],
            [(y // d) % 2 == 1 for d in doubled(n_y)],
        )
    )
    own_rows = hidden // n_loop
    half = block // CORES
    first = half * 3 // 5 // 128 * 128

    live = lax.broadcasted_iota(jnp.int32, (rows, 1), 0) < counts[0, 0]
    entries = lax.axis_size("mod") * hidden * block

    early_other, masked, late_columns, own_columns = first_term(
        counts, core, tokens, upstream, half, first
    )
    early_other = swap(early_other, "line", 1)
    (late_other,) = terms(masked, late_columns, half - first)
    late_other = swap(late_other, "line", 1)
    early, late = terms(masked, own_columns, first, half - first)
    early = early + early_other
    late = late + late_other
    back = lax.dot_general(
        after(upstream, late), weight, (((1,), (1,)), ((), ())), preferred_element_type=jnp.float32
    )
    hidden_grad = jnp.where(live, back, jnp.zeros_like(back)).astype(jnp.bfloat16)

    early = early.reshape(n_loop, n_y, own_rows // n_y, first).transpose(1, 0, 2, 3)
    early = scatter_sum(early, "line", over_y, CORES)
    late = scatter_sum(late.reshape(n_loop, own_rows, half - first), "loop", over_z)
    early_part = early
    early = scatter_sum(early, "loop", over_z)
    late = after(late, early_part)
    for d in doubled(n_y):
        late = late + swap(late, "line", d * CORES)

    squares = jnp.sum(early * early, axis=0).reshape(-1, 128).sum(0)
    squares_late = jnp.sum(late * late, axis=0).reshape(-1, 128).sum(0)
    total = (squares + jnp.where(low_y, squares_late, 0.0)).reshape(1, 128)
    total = after(total, hidden_grad)
    for d in doubled(CORES):
        total = total + swap(total, "line", d)
    spread = total
    for d in doubled(n_loop):
        total = total + swap(total, "loop", d)
    for d in doubled(lax.axis_size("mod")):
        total = total + swap(total, "mod", d)
    over_towers = total
    for d in doubled(n_y):
        total = total + swap(total, "line", d * CORES)
    factor = 1.0 / jnp.sqrt(jnp.sum(total) / entries + 1e-06)

    early = after(early, spread)[None]
    for d, is_upper in zip(doubled(n_y), upper):
        other = after(swap(early, "line", d * CORES), over_towers)
        early = jnp.where(
            is_upper, jnp.concatenate([other, early]), jnp.concatenate([early, other])
        )
    mine = jnp.concatenate([early.reshape(own_rows, first), late], axis=1)
    other = swap(mine, "line", 1)
    share = jnp.where(
        low_core,
        jnp.concatenate([mine, other], axis=1),
        jnp.concatenate([other, mine], axis=1),
    )
    clipped = share * factor

    return (clipped[None], hidden_grad[None])


def solution(mesh):
    in_specs = (
        P("mod", ("loop", "line"), None),
        P("mod", ("loop", "line"), None),
        P("mod", None, None),
        P("mod", "loop", "line"),
    )
    out_specs = (P("mod", "loop", None), P("mod", ("loop", "line"), None))
    return jax.shard_map(
        on_device, mesh=mesh, in_specs=in_specs, out_specs=out_specs, check_vma=False
    )
```

```python
import functools

import jax
import jax.numpy as jnp
from jax import lax
from jax.experimental import pallas as pl
from jax.experimental.pallas import tpu as pltpu
from jax.sharding import PartitionSpec as P

CORES = 2
VMEM_BYTES = 12 * 2**20


def swap(x, axis, distance):
    size = lax.axis_size(axis)
    return lax.ppermute(x, axis, [(i, i ^ distance) for i in range(size)])


def doubled(size):
    distance = 1
    while distance < size:
        yield distance
        distance *= 2


def after(x, *ready):
    return lax.optimization_barrier((x, *ready))[0]


def piece(x, index):
    return lax.dynamic_index_in_dim(x, index, 0, keepdims=False)


def scatter_sum(x, axis, index, stride=1):
    size = x.shape[0]
    order = sorted(range(1, size), key=lambda d: -(d ^ 1))
    got = [swap(piece(x, index[d]), axis, d * stride) for d in order]
    total = piece(x, index[0])
    for part in got:
        total = total + part
    return total


def product(left, right):
    return lax.dot_general(
        left, right, (((0,), (0,)), ((), ())), preferred_element_type=jnp.float32
    )


def first_kernel(count, place, act, dy, out, masked, late, own, tokens, early, sems):
    half = own.shape[1]
    first = early.shape[1]
    core = place[0] % CORES
    other = pl.multiple_of((1 - core) * half, 128)
    mine = pl.multiple_of(core * half, 128)
    copies = [
        pltpu.make_async_copy(act, tokens, sems.at[0]),
        pltpu.make_async_copy(dy.at[:, pl.ds(other, first)], early, sems.at[1]),
        pltpu.make_async_copy(dy.at[:, pl.ds(other + first, half - first)], late, sems.at[2]),
        pltpu.make_async_copy(dy.at[:, pl.ds(mine, half)], own, sems.at[3]),
    ]
    for copy in copies:
        copy.start()
    copies[0].wait()
    live = lax.broadcasted_iota(jnp.int32, (act.shape[0], 1), 0) < count[0, 0, 0]
    masked[...] = jnp.where(live, tokens[...], jnp.zeros_like(tokens))
    copies[1].wait()
    out[...] = product(masked[...], early[...])
    copies[2].wait()
    copies[3].wait()


def first_term(counts, place, act, dy, half, first):
    rows, hidden = act.shape
    smem = pl.BlockSpec(memory_space=pltpu.SMEM)
    vmem = pl.BlockSpec(memory_space=pltpu.VMEM)
    hbm = pl.BlockSpec(memory_space=pltpu.HBM)
    return pl.pallas_call(
        first_kernel,
        out_shape=(
            jax.ShapeDtypeStruct((hidden, first), jnp.float32),
            jax.ShapeDtypeStruct((rows, hidden), act.dtype),
            jax.ShapeDtypeStruct((rows, half - first), dy.dtype),
            jax.ShapeDtypeStruct((rows, half), dy.dtype),
        ),
        in_specs=[smem, smem, hbm, hbm],
        out_specs=(vmem,) * 4,
        scratch_shapes=[
            pltpu.VMEM((rows, hidden), act.dtype),
            pltpu.VMEM((rows, first), dy.dtype),
            pltpu.SemaphoreType.DMA((4,)),
        ],
        compiler_params=pltpu.CompilerParams(vmem_limit_bytes=VMEM_BYTES),
    )(
        counts,
        place,
        pltpu.with_memory_space_constraint(act, pltpu.HBM),
        pltpu.with_memory_space_constraint(dy, pltpu.HBM),
    )


def terms_kernel(masked, columns, *outs):
    start = 0
    for out in outs:
        width = out.shape[1]
        out[...] = product(masked[...], columns[:, start : start + width])
        start += width


def terms(masked, columns, *widths):
    vmem = pl.BlockSpec(memory_space=pltpu.VMEM)
    hidden = masked.shape[1]
    return pl.pallas_call(
        terms_kernel,
        out_shape=tuple(jax.ShapeDtypeStruct((hidden, w), jnp.float32) for w in widths),
        in_specs=[vmem, vmem],
        out_specs=(vmem,) * len(widths),
        compiler_params=pltpu.CompilerParams(vmem_limit_bytes=VMEM_BYTES),
    )(masked, columns)


def scaled_kernel(entries, place, totals, *refs):
    *pieces, out, ordered = refs
    rows, block = out.shape
    half = block // CORES
    first = pieces[0].shape[1]
    lates, earlies = pieces[-CORES:], pieces[:-CORES]
    factor = 1.0 / jnp.sqrt(jnp.sum(totals[...]) / entries + 1e-06)
    height = rows // (len(earlies) // CORES)
    for d, piece in enumerate(earlies):
        ordered[place[0] ^ d] = piece[...] * factor
    for member in range(len(earlies)):
        row, column = member // CORES * height, member % CORES * half
        out[row : row + height, column : column + first] = ordered[member]
    for d, piece in enumerate(lates):
        column = pl.multiple_of((place[0] ^ d) % CORES * half + first, 128)
        out[:, pl.ds(column, half - first)] = piece[...] * factor


def scaled(place, totals, early, late, entries):
    smem = pl.BlockSpec(memory_space=pltpu.SMEM)
    vmem = pl.BlockSpec(memory_space=pltpu.VMEM)
    rows = late[0].shape[0]
    block = CORES * (early[0].shape[1] + late[0].shape[1])
    return pl.pallas_call(
        functools.partial(scaled_kernel, entries),
        out_shape=jax.ShapeDtypeStruct((rows, block), jnp.float32),
        in_specs=[smem] + [vmem] * (1 + len(early) + len(late)),
        out_specs=vmem,
        scratch_shapes=[pltpu.VMEM((len(early), *early[0].shape), jnp.float32)],
        compiler_params=pltpu.CompilerParams(vmem_limit_bytes=VMEM_BYTES),
    )(place, totals.reshape(-1, 128), *early, *late)


def on_device(act, dy, w_out, counts):
    tokens = act[0]
    upstream = dy[0]
    weight = w_out[0]
    rows, hidden = tokens.shape
    block = weight.shape[1]
    n_loop = lax.axis_size("loop")
    n_y = lax.axis_size("line") // CORES
    z = lax.axis_index("loop").astype(jnp.uint32)
    line = lax.axis_index("line").astype(jnp.uint32)
    y = line // CORES
    place, low_y, over_z, over_y = lax.optimization_barrier(
        (
            line.astype(jnp.int32).reshape(1),
            y == 0,
            [z ^ d for d in range(n_loop)],
            [y ^ d for d in range(n_y)],
        )
    )
    own_rows = hidden // n_loop
    half = block // CORES
    first = half * 3 // 5 // 128 * 128

    live = lax.broadcasted_iota(jnp.int32, (rows, 1), 0) < counts[0, 0]
    entries = lax.axis_size("mod") * hidden * block

    early_other, masked, late_columns, own_columns = first_term(
        counts, place, tokens, upstream, half, first
    )
    early_other = swap(early_other, "line", 1)
    (late_other,) = terms(masked, late_columns, half - first)
    late_other = swap(late_other, "line", 1)
    early, late = terms(masked, own_columns, first, half - first)
    early = early + early_other
    late = late + after(late_other, early)
    back = lax.dot_general(
        after(upstream, late), weight, (((1,), (1,)), ((), ())), preferred_element_type=jnp.float32
    )
    hidden_grad = jnp.where(live, back, jnp.zeros_like(back)).astype(jnp.bfloat16)

    early = early.reshape(n_loop, n_y, own_rows // n_y, first).transpose(1, 0, 2, 3)
    early = scatter_sum(early, "line", over_y, CORES)
    late = scatter_sum(late.reshape(n_loop, own_rows, half - first), "loop", over_z)
    early_part = early
    early = scatter_sum(early, "loop", over_z)
    late = after(late, early_part)
    for d in doubled(n_y):
        late = late + swap(late, "line", d * CORES)

    squares = jnp.sum(early * early, axis=0).reshape(-1, 128).sum(0)
    squares_late = jnp.sum(late * late, axis=0).reshape(-1, 128).sum(0)
    total = (squares + jnp.where(low_y, squares_late, 0.0)).reshape(1, 128)
    total = after(total, hidden_grad)
    everyone = ("mod", "loop", "line")
    members = lax.axis_size(everyone)
    early = [early] + [swap(early, "line", d) for d in range(1, n_y * CORES)]
    late = [late] + [swap(late, "line", d) for d in range(1, CORES)]
    totals = lax.all_to_all(
        jnp.broadcast_to(total[None], (members, 1, 128)), everyone, 0, 0, tiled=True
    )
    clipped = scaled(place, totals, early, late, entries)
    return (clipped[None], hidden_grad[None])


def solution(mesh):
    in_specs = (
        P("mod", ("loop", "line"), None),
        P("mod", ("loop", "line"), None),
        P("mod", None, None),
        P("mod", "loop", "line"),
    )
    out_specs = (P("mod", "loop", None), P("mod", ("loop", "line"), None))
    return jax.shard_map(
        on_device, mesh=mesh, in_specs=in_specs, out_specs=out_specs, check_vma=False
    )
```

```python
import functools

import jax
import jax.numpy as jnp
from jax import lax
from jax.experimental import pallas as pl
from jax.experimental.pallas import tpu as pltpu
from jax.sharding import PartitionSpec as P

CORES = 2
VMEM_BYTES = 12 * 2**20


def swap(x, axis, distance):
    size = lax.axis_size(axis)
    return lax.ppermute(x, axis, [(i, i ^ distance) for i in range(size)])


def doubled(size):
    distance = 1
    while distance < size:
        yield distance
        distance *= 2


def after(x, *ready):
    return lax.optimization_barrier((x, *ready))[0]


def piece(x, index):
    return lax.dynamic_index_in_dim(x, index, 0, keepdims=False)


def farthest_first(size):
    return sorted(range(1, size), key=lambda d: -(d ^ 1))


def parcels(x, index):
    return {d: piece(x, index[d]) for d in farthest_first(x.shape[0])}


def exchanged(sends, axis, stride=1):
    return [swap(x, axis, d * stride) for d, x in sends.items()]


def summed(own, parts):
    for part in parts:
        own = own + part
    return own


def product(left, right):
    return lax.dot_general(
        left, right, (((0,), (0,)), ((), ())), preferred_element_type=jnp.float32
    )


def first_kernel(count, place, act, dy, out, masked, late, own, tokens, early, sems):
    half = own.shape[1]
    first = early.shape[1]
    core = place[0] % CORES
    other = pl.multiple_of((1 - core) * half, 128)
    mine = pl.multiple_of(core * half, 128)
    copies = [
        pltpu.make_async_copy(act, tokens, sems.at[0]),
        pltpu.make_async_copy(dy.at[:, pl.ds(other, first)], early, sems.at[1]),
        pltpu.make_async_copy(dy.at[:, pl.ds(other + first, half - first)], late, sems.at[2]),
        pltpu.make_async_copy(dy.at[:, pl.ds(mine, half)], own, sems.at[3]),
    ]
    for copy in copies:
        copy.start()
    copies[0].wait()
    live = lax.broadcasted_iota(jnp.int32, (act.shape[0], 1), 0) < count[0, 0, 0]
    masked[...] = jnp.where(live, tokens[...], jnp.zeros_like(tokens))
    copies[1].wait()
    out[...] = product(masked[...], early[...])
    copies[2].wait()
    copies[3].wait()


def first_term(counts, place, act, dy, half, first):
    rows, hidden = act.shape
    smem = pl.BlockSpec(memory_space=pltpu.SMEM)
    vmem = pl.BlockSpec(memory_space=pltpu.VMEM)
    hbm = pl.BlockSpec(memory_space=pltpu.HBM)
    return pl.pallas_call(
        first_kernel,
        out_shape=(
            jax.ShapeDtypeStruct((hidden, first), jnp.float32),
            jax.ShapeDtypeStruct((rows, hidden), act.dtype),
            jax.ShapeDtypeStruct((rows, half - first), dy.dtype),
            jax.ShapeDtypeStruct((rows, half), dy.dtype),
        ),
        in_specs=[smem, smem, hbm, hbm],
        out_specs=(vmem,) * 4,
        scratch_shapes=[
            pltpu.VMEM((rows, hidden), act.dtype),
            pltpu.VMEM((rows, first), dy.dtype),
            pltpu.SemaphoreType.DMA((4,)),
        ],
        compiler_params=pltpu.CompilerParams(vmem_limit_bytes=VMEM_BYTES),
    )(
        counts,
        place,
        pltpu.with_memory_space_constraint(act, pltpu.HBM),
        pltpu.with_memory_space_constraint(dy, pltpu.HBM),
    )


def terms_kernel(masked, columns, *outs):
    start = 0
    for out in outs:
        width = out.shape[1]
        out[...] = product(masked[...], columns[:, start : start + width])
        start += width


def terms(masked, columns, *widths):
    vmem = pl.BlockSpec(memory_space=pltpu.VMEM)
    hidden = masked.shape[1]
    return pl.pallas_call(
        terms_kernel,
        out_shape=tuple(jax.ShapeDtypeStruct((hidden, w), jnp.float32) for w in widths),
        in_specs=[vmem, vmem],
        out_specs=(vmem,) * len(widths),
        compiler_params=pltpu.CompilerParams(vmem_limit_bytes=VMEM_BYTES),
    )(masked, columns)


def scaled_kernel(entries, side, place, totals, late, early, parcel, *refs):
    *far, out, ordered = refs
    rows, block = out.shape
    half = block // CORES
    middle = late.shape[1]
    height, width = early.shape
    factor = 1.0 / jnp.sqrt(jnp.sum(totals[...]) / entries + 1e-06)
    pieces = [early[...], parcel[:, :width], *(x[...] for x in far)]
    for d, x in enumerate(pieces):
        ordered[place[0] ^ d] = x * factor
    for member in range(len(pieces)):
        row, column = member // CORES * height, member % CORES * half
        out[row : row + height, column : column + side] = ordered[member, :, :side]
        column += side + middle
        out[row : row + height, column : column + width - side] = ordered[member, :, side:]
    core = place[0] % CORES
    mine = pl.multiple_of(core * half + side, 128)
    other = pl.multiple_of((1 - core) * half + side, 128)
    out[:, pl.ds(mine, middle)] = late[...] * factor
    for part in range(rows // height):
        start = width + part * middle
        x = parcel[:, start : start + middle] * factor
        out[part * height : (part + 1) * height, pl.ds(other, middle)] = x


def scaled(place, totals, late, early, parcel, far, side, entries):
    smem = pl.BlockSpec(memory_space=pltpu.SMEM)
    vmem = pl.BlockSpec(memory_space=pltpu.VMEM)
    rows, middle = late.shape
    height, width = early.shape
    return pl.pallas_call(
        functools.partial(scaled_kernel, entries, side),
        out_shape=jax.ShapeDtypeStruct((rows, CORES * (width + middle)), jnp.float32),
        in_specs=[smem] + [vmem] * (4 + len(far)),
        out_specs=vmem,
        scratch_shapes=[pltpu.VMEM((CORES + len(far), height, width), jnp.float32)],
        compiler_params=pltpu.CompilerParams(vmem_limit_bytes=VMEM_BYTES),
    )(place, totals.reshape(-1, 128), late, early, parcel, *far)


def on_device(act, dy, w_out, counts):
    tokens = act[0]
    upstream = dy[0]
    weight = w_out[0]
    rows, hidden = tokens.shape
    block = weight.shape[1]
    n_loop = lax.axis_size("loop")
    n_y = lax.axis_size("line") // CORES
    z = lax.axis_index("loop").astype(jnp.uint32)
    line = lax.axis_index("line").astype(jnp.uint32)
    y = line // CORES
    place, low_y, over_z, over_y = lax.optimization_barrier(
        (
            line.astype(jnp.int32).reshape(1),
            y == 0,
            [z ^ d for d in range(n_loop)],
            [y ^ d for d in range(n_y)],
        )
    )
    own_rows = hidden // n_loop
    half = block // CORES
    tile = half // 5 // 128 * 128
    widths = (2 * tile, 2 * tile, half - 4 * tile)

    live = lax.broadcasted_iota(jnp.int32, (rows, 1), 0) < counts[0, 0]
    entries = lax.axis_size("mod") * hidden * block

    def by_row_part(x):
        return x.reshape(n_loop, n_y, own_rows // n_y, -1).transpose(1, 0, 2, 3)

    first_other, masked, columns, own_columns = first_term(
        counts, place, tokens, upstream, half, widths[0]
    )
    first_other = swap(first_other, "line", 1)
    late_other, second_other = terms(masked, columns, *widths[1:])
    late_other = swap(late_other, "line", 1)
    second_other = swap(second_other, "line", 1)
    first_sum, late, second_sum = terms(masked, own_columns, *widths)
    first_sum = by_row_part(first_sum + first_other)
    sends = parcels(first_sum, over_y)
    first_parts = exchanged(sends, "line", CORES)
    late = late + after(late_other, *sends.values())
    late = late.reshape(n_loop, own_rows, widths[1])
    sends = parcels(late, over_z)
    late_parts = exchanged(sends, "loop")
    second_sum = by_row_part(second_sum + after(second_other, *sends.values()))
    sends = parcels(second_sum, over_y)
    second_parts = exchanged(sends, "line", CORES)
    first_parts = [after(part, *sends.values()) for part in first_parts]
    back = lax.dot_general(
        after(upstream, *sends.values()),
        weight,
        (((1,), (1,)), ((), ())),
        preferred_element_type=jnp.float32,
    )
    hidden_grad = jnp.where(live, back, jnp.zeros_like(back)).astype(jnp.bfloat16)

    early = jnp.concatenate(
        [
            summed(piece(x, over_y[0]), parts)
            for x, parts in ((first_sum, first_parts), (second_sum, second_parts))
        ],
        axis=-1,
    )
    sends = parcels(early, over_z)
    early_parts = exchanged(sends, "loop")
    late_parts = [after(part, *sends.values()) for part in late_parts]
    late = summed(piece(late, over_z[0]), late_parts)
    late = after(late, *sends.values())
    for d in doubled(n_y):
        late = late + swap(late, "line", d * CORES)
    early = summed(piece(early, over_z[0]), early_parts)

    squares = jnp.sum(early * early, axis=0).reshape(-1, 128).sum(0)
    squares_late = jnp.sum(late * late, axis=0).reshape(-1, 128).sum(0)
    total = (squares + jnp.where(low_y, squares_late, 0.0)).reshape(1, 128)
    total = after(total, hidden_grad)
    height = own_rows // n_y
    rows_late = [late[start : start + height] for start in range(0, own_rows, height)]
    parcel = swap(jnp.concatenate([early, *rows_late], axis=1), "line", 1)
    far = [swap(early, "line", d) for d in range(CORES, n_y * CORES)]
    everyone = ("mod", "loop", "line")
    members = lax.axis_size(everyone)
    totals = lax.all_to_all(
        jnp.broadcast_to(total[None], (members, 1, 128)), everyone, 0, 0, tiled=True
    )
    clipped = scaled(place, totals, late, early, parcel, far, widths[0], entries)
    return (clipped[None], hidden_grad[None])


def solution(mesh):
    in_specs = (
        P("mod", ("loop", "line"), None),
        P("mod", ("loop", "line"), None),
        P("mod", None, None),
        P("mod", "loop", "line"),
    )
    out_specs = (P("mod", "loop", None), P("mod", ("loop", "line"), None))
    return jax.shard_map(
        on_device, mesh=mesh, in_specs=in_specs, out_specs=out_specs, check_vma=False
    )
```

```python
import functools

import jax
import jax.numpy as jnp
from jax import lax
from jax.experimental import pallas as pl
from jax.experimental.pallas import tpu as pltpu
from jax.sharding import PartitionSpec as P

CORES = 2
VMEM_BYTES = 12 * 2**20


def swap(x, axis, distance):
    size = lax.axis_size(axis)
    return lax.ppermute(x, axis, [(i, i ^ distance) for i in range(size)])


def doubled(size):
    distance = 1
    while distance < size:
        yield distance
        distance *= 2


def after(x, *ready):
    return lax.optimization_barrier((x, *ready))[0]


def piece(x, index):
    return lax.dynamic_index_in_dim(x, index, 0, keepdims=False)


def farthest_first(size):
    return sorted(range(1, size), key=lambda d: -(d ^ 1))


def parcels(x, index):
    return {d: piece(x, index[d]) for d in farthest_first(x.shape[0])}


def exchanged(sends, axis, stride=1):
    return [swap(x, axis, d * stride) for d, x in sends.items()]


def summed(own, parts):
    for part in parts:
        own = own + part
    return own


def product(left, right):
    return lax.dot_general(
        left, right, (((0,), (0,)), ((), ())), preferred_element_type=jnp.float32
    )


def first_kernel(widths, count, place, act, dy, out, masked, x, y, tokens, middle_dy, sems):
    side, middle, last = widths
    core = place[0] % CORES
    other = pl.multiple_of((1 - core) * sum(widths), 128)
    mine = pl.multiple_of(core * sum(widths), 128)
    moves = [
        (other + side, middle_dy, 0, middle),
        (other, x, 0, side),
        (mine + side, x, side, middle),
        (mine, y, 0, side),
        (other + side + middle, y, side, last),
        (mine + side + middle, y, side + last, last),
    ]
    copies = [pltpu.make_async_copy(act, tokens, sems.at[0])]
    for column, target, start, width in moves:
        source = dy.at[:, pl.ds(column, width)]
        target = target.at[:, start : start + width]
        copies.append(pltpu.make_async_copy(source, target, sems.at[len(copies)]))
    for copy in copies:
        copy.start()
    copies[0].wait()
    live = lax.broadcasted_iota(jnp.int32, (act.shape[0], 1), 0) < count[0, 0, 0]
    masked[...] = jnp.where(live, tokens[...], jnp.zeros_like(tokens))
    copies[1].wait()
    out[...] = product(masked[...], middle_dy[...])
    for copy in copies[2:]:
        copy.wait()


def first_term(counts, place, act, dy, widths):
    rows, hidden = act.shape
    side, middle, last = widths
    smem = pl.BlockSpec(memory_space=pltpu.SMEM)
    vmem = pl.BlockSpec(memory_space=pltpu.VMEM)
    hbm = pl.BlockSpec(memory_space=pltpu.HBM)
    return pl.pallas_call(
        functools.partial(first_kernel, widths),
        out_shape=(
            jax.ShapeDtypeStruct((hidden, middle), jnp.float32),
            jax.ShapeDtypeStruct((rows, hidden), act.dtype),
            jax.ShapeDtypeStruct((rows, side + middle), dy.dtype),
            jax.ShapeDtypeStruct((rows, side + 2 * last), dy.dtype),
        ),
        in_specs=[smem, smem, hbm, hbm],
        out_specs=(vmem,) * 4,
        scratch_shapes=[
            pltpu.VMEM((rows, hidden), act.dtype),
            pltpu.VMEM((rows, middle), dy.dtype),
            pltpu.SemaphoreType.DMA((7,)),
        ],
        compiler_params=pltpu.CompilerParams(vmem_limit_bytes=VMEM_BYTES),
    )(
        counts,
        place,
        pltpu.with_memory_space_constraint(act, pltpu.HBM),
        pltpu.with_memory_space_constraint(dy, pltpu.HBM),
    )


def terms_kernel(masked, columns, *outs):
    start = 0
    for out in outs:
        width = out.shape[1]
        out[...] = product(masked[...], columns[:, start : start + width])
        start += width


def terms(masked, columns, *widths):
    vmem = pl.BlockSpec(memory_space=pltpu.VMEM)
    hidden = masked.shape[1]
    return pl.pallas_call(
        terms_kernel,
        out_shape=tuple(jax.ShapeDtypeStruct((hidden, w), jnp.float32) for w in widths),
        in_specs=[vmem, vmem],
        out_specs=(vmem,) * len(widths),
        compiler_params=pltpu.CompilerParams(vmem_limit_bytes=VMEM_BYTES),
    )(masked, columns)


def scaled_kernel(entries, side, place, totals, late, early, parcel, *refs):
    *far, out, ordered = refs
    rows, block = out.shape
    half = block // CORES
    middle = late.shape[1]
    height, width = early.shape
    factor = 1.0 / jnp.sqrt(jnp.sum(totals[...]) / entries + 1e-06)
    pieces = [early[...], parcel[:, :width], *(x[...] for x in far)]
    for d, x in enumerate(pieces):
        ordered[place[0] ^ d] = x * factor
    for member in range(len(pieces)):
        row, column = member // CORES * height, member % CORES * half
        out[row : row + height, column : column + side] = ordered[member, :, :side]
        column += side + middle
        out[row : row + height, column : column + width - side] = ordered[member, :, side:]
    core = place[0] % CORES
    mine = pl.multiple_of(core * half + side, 128)
    other = pl.multiple_of((1 - core) * half + side, 128)
    out[:, pl.ds(mine, middle)] = late[...] * factor
    for part in range(rows // height):
        start = width + part * middle
        x = parcel[:, start : start + middle] * factor
        out[part * height : (part + 1) * height, pl.ds(other, middle)] = x


def scaled(place, totals, late, early, parcel, far, side, entries):
    smem = pl.BlockSpec(memory_space=pltpu.SMEM)
    vmem = pl.BlockSpec(memory_space=pltpu.VMEM)
    rows, middle = late.shape
    height, width = early.shape
    return pl.pallas_call(
        functools.partial(scaled_kernel, entries, side),
        out_shape=jax.ShapeDtypeStruct((rows, CORES * (width + middle)), jnp.float32),
        in_specs=[smem] + [vmem] * (4 + len(far)),
        out_specs=vmem,
        scratch_shapes=[pltpu.VMEM((CORES + len(far), height, width), jnp.float32)],
        compiler_params=pltpu.CompilerParams(vmem_limit_bytes=VMEM_BYTES),
    )(place, totals.reshape(-1, 128), late, early, parcel, *far)


def on_device(act, dy, w_out, counts):
    tokens = act[0]
    upstream = dy[0]
    weight = w_out[0]
    rows, hidden = tokens.shape
    block = weight.shape[1]
    n_loop = lax.axis_size("loop")
    n_y = lax.axis_size("line") // CORES
    z = lax.axis_index("loop").astype(jnp.uint32)
    line = lax.axis_index("line").astype(jnp.uint32)
    y = line // CORES
    place, low_y, over_z, over_y = lax.optimization_barrier(
        (
            line.astype(jnp.int32).reshape(1),
            y == 0,
            [z ^ d for d in range(n_loop)],
            [y ^ d for d in range(n_y)],
        )
    )
    own_rows = hidden // n_loop
    half = block // CORES
    tile = half // 5 // 128 * 128
    widths = (2 * tile, 2 * tile, half - 4 * tile)

    live = lax.broadcasted_iota(jnp.int32, (rows, 1), 0) < counts[0, 0]
    entries = lax.axis_size("mod") * hidden * block

    def by_row_part(x):
        return x.reshape(n_loop, n_y, own_rows // n_y, -1).transpose(1, 0, 2, 3)

    late_other, masked, columns, more_columns = first_term(
        counts, place, tokens, upstream, widths
    )
    late_other = swap(late_other, "line", 1)
    first_other, late = terms(masked, columns, *widths[:2])
    first_other = swap(first_other, "line", 1)
    first_sum, second_both = terms(masked, more_columns, widths[0], 2 * widths[2])
    second_other, second_sum = second_both[:, : widths[2]], second_both[:, widths[2] :]
    second_other = swap(second_other, "line", 1)
    late = (late + late_other).reshape(n_loop, own_rows, widths[1])
    late_sends = parcels(late, over_z)
    farthest, *others = late_sends
    first_sum = by_row_part(first_sum + after(first_other, late_sends[farthest]))
    sends = parcels(first_sum, over_y)
    first_parts = exchanged(sends, "line", CORES)
    late_parts = exchanged(late_sends, "loop")
    second_sum = by_row_part(second_sum + after(second_other, *late_sends.values(), *sends.values()))
    sends = parcels(second_sum, over_y)
    second_parts = exchanged(sends, "line", CORES)
    first_parts = [after(part, *sends.values()) for part in first_parts]
    back = lax.dot_general(
        after(upstream, *sends.values()),
        weight,
        (((1,), (1,)), ((), ())),
        preferred_element_type=jnp.float32,
    )
    hidden_grad = jnp.where(live, back, jnp.zeros_like(back)).astype(jnp.bfloat16)

    early = jnp.concatenate(
        [
            summed(piece(x, over_y[0]), parts)
            for x, parts in ((first_sum, first_parts), (second_sum, second_parts))
        ],
        axis=-1,
    )
    sends = parcels(early, over_z)
    early_parts = exchanged(sends, "loop")
    late_parts = [after(part, *sends.values()) for part in late_parts]
    late = summed(piece(late, over_z[0]), late_parts)
    late = after(late, *sends.values())
    for d in doubled(n_y):
        late = late + swap(late, "line", d * CORES)
    early = summed(piece(early, over_z[0]), early_parts)

    squares = jnp.sum(early * early, axis=0).reshape(-1, 128).sum(0)
    squares_late = jnp.sum(late * late, axis=0).reshape(-1, 128).sum(0)
    total = (squares + jnp.where(low_y, squares_late, 0.0)).reshape(1, 128)
    total = after(total, hidden_grad)
    height = own_rows // n_y
    rows_late = [late[start : start + height] for start in range(0, own_rows, height)]
    parcel = swap(jnp.concatenate([early, *rows_late], axis=1), "line", 1)
    far = [swap(early, "line", d) for d in range(CORES, n_y * CORES)]
    everyone = ("mod", "loop", "line")
    members = lax.axis_size(everyone)
    totals = lax.all_to_all(
        jnp.broadcast_to(total[None], (members, 1, 128)), everyone, 0, 0, tiled=True
    )
    clipped = scaled(place, totals, late, early, parcel, far, widths[0], entries)
    return (clipped[None], hidden_grad[None])


def solution(mesh):
    in_specs = (
        P("mod", ("loop", "line"), None),
        P("mod", ("loop", "line"), None),
        P("mod", None, None),
        P("mod", "loop", "line"),
    )
    out_specs = (P("mod", "loop", None), P("mod", ("loop", "line"), None))
    return jax.shard_map(
        on_device, mesh=mesh, in_specs=in_specs, out_specs=out_specs, check_vma=False
    )
```

```python
import functools

import jax
import jax.numpy as jnp
from jax import lax
from jax.experimental import pallas as pl
from jax.experimental.pallas import tpu as pltpu
from jax.sharding import PartitionSpec as P

CORES = 2
VMEM_BYTES = 12 * 2**20


def swap(x, axis, distance):
    size = lax.axis_size(axis)
    return lax.ppermute(x, axis, [(i, i ^ distance) for i in range(size)])


def doubled(size):
    distance = 1
    while distance < size:
        yield distance
        distance *= 2


def after(x, *ready):
    return lax.optimization_barrier((x, *ready))[0]


def piece(x, index):
    return lax.dynamic_index_in_dim(x, index, 0, keepdims=False)


def farthest_first(size):
    return sorted(range(1, size), key=lambda d: -(d ^ 1))


def parcels(x, index):
    return {d: piece(x, index[d]) for d in farthest_first(x.shape[0])}


def exchanged(sends, axis, stride=1):
    return [swap(x, axis, d * stride) for d, x in sends.items()]


def summed(own, parts):
    for part in parts:
        own = own + part
    return own


def product(left, right):
    return lax.dot_general(
        left, right, (((0,), (0,)), ((), ())), preferred_element_type=jnp.float32
    )


def first_kernel(start, count, place, act, dy, out, masked, tokens, columns, sems):
    width = columns.shape[1]
    half = dy.shape[1] // CORES
    column = pl.multiple_of((1 - place[0] % CORES) * half + start, 128)
    copies = [
        pltpu.make_async_copy(act, tokens, sems.at[0]),
        pltpu.make_async_copy(dy.at[:, pl.ds(column, width)], columns, sems.at[1]),
    ]
    for copy in copies:
        copy.start()
    copies[0].wait()
    live = lax.broadcasted_iota(jnp.int32, (act.shape[0], 1), 0) < count[0, 0, 0]
    masked[...] = jnp.where(live, tokens[...], jnp.zeros_like(tokens))
    copies[1].wait()
    out[...] = product(masked[...], columns[...])


def first_term(counts, place, act, dy, start, width):
    rows, hidden = act.shape
    smem = pl.BlockSpec(memory_space=pltpu.SMEM)
    vmem = pl.BlockSpec(memory_space=pltpu.VMEM)
    hbm = pl.BlockSpec(memory_space=pltpu.HBM)
    return pl.pallas_call(
        functools.partial(first_kernel, start),
        out_shape=(
            jax.ShapeDtypeStruct((hidden, width), jnp.float32),
            jax.ShapeDtypeStruct((rows, hidden), act.dtype),
        ),
        in_specs=[smem, smem, hbm, hbm],
        out_specs=(vmem,) * 2,
        scratch_shapes=[
            pltpu.VMEM((rows, hidden), act.dtype),
            pltpu.VMEM((rows, width), dy.dtype),
            pltpu.SemaphoreType.DMA((2,)),
        ],
        compiler_params=pltpu.CompilerParams(vmem_limit_bytes=VMEM_BYTES),
    )(
        counts,
        place,
        pltpu.with_memory_space_constraint(act, pltpu.HBM),
        pltpu.with_memory_space_constraint(dy, pltpu.HBM),
    )


def terms_kernel(spans, place, masked, dy, *outs):
    half = dy.shape[1] // CORES
    core = place[0] % CORES
    for (own, start), out in zip(spans, outs):
        column = pl.multiple_of((core if own else 1 - core) * half + start, 128)
        out[...] = product(masked[...], dy[:, pl.ds(column, out.shape[1])])


def terms(place, masked, dy, *spans):
    vmem = pl.BlockSpec(memory_space=pltpu.VMEM)
    hidden = masked.shape[1]
    return pl.pallas_call(
        functools.partial(terms_kernel, [span[:2] for span in spans]),
        out_shape=tuple(jax.ShapeDtypeStruct((hidden, span[2]), jnp.float32) for span in spans),
        in_specs=[pl.BlockSpec(memory_space=pltpu.SMEM), vmem, vmem],
        out_specs=(vmem,) * len(spans),
        compiler_params=pltpu.CompilerParams(vmem_limit_bytes=VMEM_BYTES),
    )(place, masked, dy)


def scaled_kernel(entries, side, place, totals, late, early, parcel, *refs):
    *far, out, ordered = refs
    rows, block = out.shape
    half = block // CORES
    middle = late.shape[1]
    height, width = early.shape
    factor = 1.0 / jnp.sqrt(jnp.sum(totals[...]) / entries + 1e-06)
    pieces = [early[...], parcel[:, :width], *(x[...] for x in far)]
    for d, x in enumerate(pieces):
        ordered[place[0] ^ d] = x * factor
    for member in range(len(pieces)):
        row, column = member // CORES * height, member % CORES * half
        out[row : row + height, column : column + side] = ordered[member, :, :side]
        column += side + middle
        out[row : row + height, column : column + width - side] = ordered[member, :, side:]
    core = place[0] % CORES
    mine = pl.multiple_of(core * half + side, 128)
    other = pl.multiple_of((1 - core) * half + side, 128)
    out[:, pl.ds(mine, middle)] = late[...] * factor
    for part in range(rows // height):
        start = width + part * middle
        x = parcel[:, start : start + middle] * factor
        out[part * height : (part + 1) * height, pl.ds(other, middle)] = x


def scaled(place, totals, late, early, parcel, far, side, entries):
    smem = pl.BlockSpec(memory_space=pltpu.SMEM)
    vmem = pl.BlockSpec(memory_space=pltpu.VMEM)
    rows, middle = late.shape
    height, width = early.shape
    return pl.pallas_call(
        functools.partial(scaled_kernel, entries, side),
        out_shape=jax.ShapeDtypeStruct((rows, CORES * (width + middle)), jnp.float32),
        in_specs=[smem] + [vmem] * (4 + len(far)),
        out_specs=vmem,
        scratch_shapes=[pltpu.VMEM((CORES + len(far), height, width), jnp.float32)],
        compiler_params=pltpu.CompilerParams(vmem_limit_bytes=VMEM_BYTES),
    )(place, totals.reshape(-1, 128), late, early, parcel, *far)


def on_device(act, dy, w_out, counts):
    tokens = act[0]
    upstream = dy[0]
    weight = w_out[0]
    rows, hidden = tokens.shape
    block = weight.shape[1]
    n_loop = lax.axis_size("loop")
    n_y = lax.axis_size("line") // CORES
    z = lax.axis_index("loop").astype(jnp.uint32)
    line = lax.axis_index("line").astype(jnp.uint32)
    y = line // CORES
    place, low_y, over_z, over_y = lax.optimization_barrier(
        (
            line.astype(jnp.int32).reshape(1),
            y == 0,
            [z ^ d for d in range(n_loop)],
            [y ^ d for d in range(n_y)],
        )
    )
    own_rows = hidden // n_loop
    half = block // CORES
    tile = half // 5 // 128 * 128
    widths = (2 * tile, 2 * tile, half - 4 * tile)

    live = lax.broadcasted_iota(jnp.int32, (rows, 1), 0) < counts[0, 0]
    entries = lax.axis_size("mod") * hidden * block

    def by_row_part(x):
        return x.reshape(n_loop, n_y, own_rows // n_y, -1).transpose(1, 0, 2, 3)

    side, middle, last = widths
    late_other, masked = first_term(counts, place, tokens, upstream, side, middle)
    late_other = swap(late_other, "line", 1)
    first_other, late = terms(
        place, masked, upstream, (False, 0, side), (True, side, middle)
    )
    first_other = swap(first_other, "line", 1)
    first_sum, second_other, second_sum = terms(
        place,
        masked,
        upstream,
        (True, 0, side),
        (False, side + middle, last),
        (True, side + middle, last),
    )
    second_other = swap(second_other, "line", 1)
    late = (late + late_other).reshape(n_loop, own_rows, widths[1])
    late_sends = parcels(late, over_z)
    farthest, *others = late_sends
    first_sum = by_row_part(first_sum + after(first_other, late_sends[farthest]))
    sends = parcels(first_sum, over_y)
    first_parts = exchanged(sends, "line", CORES)
    late_parts = exchanged(late_sends, "loop")
    second_sum = by_row_part(second_sum + after(second_other, *late_sends.values(), *sends.values()))
    sends = parcels(second_sum, over_y)
    second_parts = exchanged(sends, "line", CORES)
    first_parts = [after(part, *sends.values()) for part in first_parts]
    back = lax.dot_general(
        after(upstream, *sends.values()),
        weight,
        (((1,), (1,)), ((), ())),
        preferred_element_type=jnp.float32,
    )
    hidden_grad = jnp.where(live, back, jnp.zeros_like(back)).astype(jnp.bfloat16)

    early = jnp.concatenate(
        [
            summed(piece(x, over_y[0]), parts)
            for x, parts in ((first_sum, first_parts), (second_sum, second_parts))
        ],
        axis=-1,
    )
    sends = parcels(early, over_z)
    early_parts = exchanged(sends, "loop")
    late_parts = [after(part, *sends.values()) for part in late_parts]
    late = summed(piece(late, over_z[0]), late_parts)
    late = after(late, *sends.values())
    for d in doubled(n_y):
        late = late + swap(late, "line", d * CORES)
    early = summed(piece(early, over_z[0]), early_parts)

    squares = jnp.sum(early * early, axis=0).reshape(-1, 128).sum(0)
    squares_late = jnp.sum(late * late, axis=0).reshape(-1, 128).sum(0)
    total = (squares + jnp.where(low_y, squares_late, 0.0)).reshape(1, 128)
    total = after(total, hidden_grad)
    height = own_rows // n_y
    rows_late = [late[start : start + height] for start in range(0, own_rows, height)]
    parcel = jnp.concatenate([early, *rows_late], axis=1)
    far = [swap(after(early, parcel), "line", d) for d in range(CORES, n_y * CORES)]
    parcel = swap(parcel, "line", 1)
    everyone = ("mod", "loop", "line")
    members = lax.axis_size(everyone)
    totals = lax.all_to_all(
        jnp.broadcast_to(total[None], (members, 1, 128)), everyone, 0, 0, tiled=True
    )
    clipped = scaled(place, totals, late, early, parcel, far, widths[0], entries)
    return (clipped[None], hidden_grad[None])


def solution(mesh):
    in_specs = (
        P("mod", ("loop", "line"), None),
        P("mod", ("loop", "line"), None),
        P("mod", None, None),
        P("mod", "loop", "line"),
    )
    out_specs = (P("mod", "loop", None), P("mod", ("loop", "line"), None))
    return jax.shard_map(
        on_device, mesh=mesh, in_specs=in_specs, out_specs=out_specs, check_vma=False
    )
```

```python
import functools

import jax
import jax.numpy as jnp
from jax import lax
from jax.experimental import pallas as pl
from jax.experimental.pallas import tpu as pltpu
from jax.sharding import PartitionSpec as P

CORES = 2
VMEM_BYTES = 12 * 2**20


def swap(x, axis, distance):
    size = lax.axis_size(axis)
    return lax.ppermute(x, axis, [(i, i ^ distance) for i in range(size)])


def doubled(size):
    distance = 1
    while distance < size:
        yield distance
        distance *= 2


def after(x, *ready):
    return lax.optimization_barrier((x, *ready))[0]


def piece(x, index):
    return lax.dynamic_index_in_dim(x, index, 0, keepdims=False)


def farthest_first(size):
    return sorted(range(1, size), key=lambda d: -(d ^ 1))


def parcels(x, index):
    return {d: piece(x, index[d]) for d in farthest_first(x.shape[0])}


def exchanged(sends, axis, stride=1):
    return [swap(x, axis, d * stride) for d, x in sends.items()]


def summed(own, parts):
    for part in parts:
        own = own + part
    return own


def product(left, right):
    return lax.dot_general(
        left, right, (((0,), (0,)), ((), ())), preferred_element_type=jnp.float32
    )


def first_kernel(start, count, place, act, dy, out, masked, tokens, columns, sems):
    width = columns.shape[1]
    half = dy.shape[1] // CORES
    column = pl.multiple_of((1 - place[0] % CORES) * half + start, 128)
    copies = [
        pltpu.make_async_copy(act, tokens, sems.at[0]),
        pltpu.make_async_copy(dy.at[:, pl.ds(column, width)], columns, sems.at[1]),
    ]
    for copy in copies:
        copy.start()
    copies[0].wait()
    live = lax.broadcasted_iota(jnp.int32, (act.shape[0], 1), 0) < count[0, 0, 0]
    masked[...] = jnp.where(live, tokens[...], jnp.zeros_like(tokens))
    copies[1].wait()
    out[...] = product(masked[...], columns[...])


def first_term(counts, place, act, dy, start, width):
    rows, hidden = act.shape
    smem = pl.BlockSpec(memory_space=pltpu.SMEM)
    vmem = pl.BlockSpec(memory_space=pltpu.VMEM)
    hbm = pl.BlockSpec(memory_space=pltpu.HBM)
    return pl.pallas_call(
        functools.partial(first_kernel, start),
        out_shape=(
            jax.ShapeDtypeStruct((hidden, width), jnp.float32),
            jax.ShapeDtypeStruct((rows, hidden), act.dtype),
        ),
        in_specs=[smem, smem, hbm, hbm],
        out_specs=(vmem,) * 2,
        scratch_shapes=[
            pltpu.VMEM((rows, hidden), act.dtype),
            pltpu.VMEM((rows, width), dy.dtype),
            pltpu.SemaphoreType.DMA((2,)),
        ],
        compiler_params=pltpu.CompilerParams(vmem_limit_bytes=VMEM_BYTES),
    )(
        counts,
        place,
        pltpu.with_memory_space_constraint(act, pltpu.HBM),
        pltpu.with_memory_space_constraint(dy, pltpu.HBM),
    )


def terms_kernel(spans, place, masked, dy, *outs):
    half = dy.shape[1] // CORES
    core = place[0] % CORES
    columns = []
    for (own, start), out in zip(spans, outs):
        column = pl.multiple_of((core if own else 1 - core) * half + start, 128)
        columns.append(dy[:, pl.ds(column, out.shape[1])])
    narrow = [i for i, out in enumerate(outs) if out.shape[1] <= 128]
    if len(narrow) == 2:
        both = product(masked[...], jnp.concatenate([columns[i] for i in narrow], axis=1))
        width = outs[narrow[0]].shape[1]
        outs[narrow[0]][...] = both[:, :width]
        outs[narrow[1]][...] = both[:, width:]
    for i, out in enumerate(outs):
        if len(narrow) != 2 or i not in narrow:
            out[...] = product(masked[...], columns[i])


def terms(place, masked, dy, *spans):
    vmem = pl.BlockSpec(memory_space=pltpu.VMEM)
    hidden = masked.shape[1]
    return pl.pallas_call(
        functools.partial(terms_kernel, [span[:2] for span in spans]),
        out_shape=tuple(jax.ShapeDtypeStruct((hidden, span[2]), jnp.float32) for span in spans),
        in_specs=[pl.BlockSpec(memory_space=pltpu.SMEM), vmem, vmem],
        out_specs=(vmem,) * len(spans),
        compiler_params=pltpu.CompilerParams(vmem_limit_bytes=VMEM_BYTES),
    )(place, masked, dy)


def scaled_kernel(entries, side, place, totals, late, early, parcel, *refs):
    *far, out, ordered = refs
    rows, block = out.shape
    half = block // CORES
    middle = late.shape[1]
    height, width = early.shape
    factor = 1.0 / jnp.sqrt(jnp.sum(totals[...]) / entries + 1e-06)
    pieces = [early[...], parcel[:, :width], *(x[...] for x in far)]
    for d, x in enumerate(pieces):
        ordered[place[0] ^ d] = x * factor
    for member in range(len(pieces)):
        row, column = member // CORES * height, member % CORES * half
        out[row : row + height, column : column + side] = ordered[member, :, :side]
        column += side + middle
        out[row : row + height, column : column + width - side] = ordered[member, :, side:]
    core = place[0] % CORES
    mine = pl.multiple_of(core * half + side, 128)
    other = pl.multiple_of((1 - core) * half + side, 128)
    out[:, pl.ds(mine, middle)] = late[...] * factor
    for part in range(rows // height):
        start = width + part * middle
        x = parcel[:, start : start + middle] * factor
        out[part * height : (part + 1) * height, pl.ds(other, middle)] = x


def scaled(place, totals, late, early, parcel, far, side, entries):
    smem = pl.BlockSpec(memory_space=pltpu.SMEM)
    vmem = pl.BlockSpec(memory_space=pltpu.VMEM)
    rows, middle = late.shape
    height, width = early.shape
    return pl.pallas_call(
        functools.partial(scaled_kernel, entries, side),
        out_shape=jax.ShapeDtypeStruct((rows, CORES * (width + middle)), jnp.float32),
        in_specs=[smem] + [vmem] * (4 + len(far)),
        out_specs=vmem,
        scratch_shapes=[pltpu.VMEM((CORES + len(far), height, width), jnp.float32)],
        compiler_params=pltpu.CompilerParams(vmem_limit_bytes=VMEM_BYTES),
    )(place, totals.reshape(-1, 128), late, early, parcel, *far)


def on_device(act, dy, w_out, counts):
    tokens = act[0]
    upstream = dy[0]
    weight = w_out[0]
    rows, hidden = tokens.shape
    block = weight.shape[1]
    n_loop = lax.axis_size("loop")
    n_y = lax.axis_size("line") // CORES
    z = lax.axis_index("loop").astype(jnp.uint32)
    line = lax.axis_index("line").astype(jnp.uint32)
    y = line // CORES
    place, low_y, over_z, over_y = lax.optimization_barrier(
        (
            line.astype(jnp.int32).reshape(1),
            y == 0,
            [z ^ d for d in range(n_loop)],
            [y ^ d for d in range(n_y)],
        )
    )
    own_rows = hidden // n_loop
    half = block // CORES
    tile = half // 5 // 128 * 128
    widths = (2 * tile, 2 * tile, half - 4 * tile)

    live = lax.broadcasted_iota(jnp.int32, (rows, 1), 0) < counts[0, 0]
    entries = lax.axis_size("mod") * hidden * block

    def by_row_part(x):
        return x.reshape(n_loop, n_y, own_rows // n_y, -1).transpose(1, 0, 2, 3)

    side, middle, last = widths
    late_other, masked = first_term(counts, place, tokens, upstream, side, middle)
    late_other = swap(late_other, "line", 1)
    first_other, late = terms(
        place, masked, upstream, (False, 0, side), (True, side, middle)
    )
    first_other = swap(first_other, "line", 1)
    first_sum, second_other, second_sum = terms(
        place,
        masked,
        upstream,
        (True, 0, side),
        (False, side + middle, last),
        (True, side + middle, last),
    )
    second_other = swap(second_other, "line", 1)
    late = (late + late_other).reshape(n_loop, own_rows, widths[1])
    late_sends = parcels(late, over_z)
    farthest, *others = late_sends
    first_sum = by_row_part(first_sum + after(first_other, late_sends[farthest]))
    sends = parcels(first_sum, over_y)
    first_parts = exchanged(sends, "line", CORES)
    late_parts = exchanged(late_sends, "loop")
    second_sum = by_row_part(second_sum + after(second_other, *late_sends.values(), *sends.values()))
    sends = parcels(second_sum, over_y)
    second_parts = exchanged(sends, "line", CORES)
    first_parts = [after(part, *sends.values()) for part in first_parts]
    back = lax.dot_general(
        after(upstream, *sends.values()),
        weight,
        (((1,), (1,)), ((), ())),
        preferred_element_type=jnp.float32,
    )
    hidden_grad = jnp.where(live, back, jnp.zeros_like(back)).astype(jnp.bfloat16)

    early = jnp.concatenate(
        [
            summed(piece(x, over_y[0]), parts)
            for x, parts in ((first_sum, first_parts), (second_sum, second_parts))
        ],
        axis=-1,
    )
    sends = parcels(early, over_z)
    early_parts = exchanged(sends, "loop")
    late_parts = [after(part, *sends.values()) for part in late_parts]
    late = summed(piece(late, over_z[0]), late_parts)
    late = after(late, *sends.values())
    for d in doubled(n_y):
        late = late + swap(late, "line", d * CORES)
    early = summed(piece(early, over_z[0]), early_parts)

    squares = jnp.sum(early * early, axis=0).reshape(-1, 128).sum(0)
    squares_late = jnp.sum(late * late, axis=0).reshape(-1, 128).sum(0)
    total = (squares + jnp.where(low_y, squares_late, 0.0)).reshape(1, 128)
    total = after(total, hidden_grad)
    height = own_rows // n_y
    rows_late = [late[start : start + height] for start in range(0, own_rows, height)]
    parcel = jnp.concatenate([early, *rows_late], axis=1)
    far = [swap(after(early, parcel), "line", d) for d in range(CORES, n_y * CORES)]
    parcel = swap(parcel, "line", 1)
    everyone = ("mod", "loop", "line")
    members = lax.axis_size(everyone)
    totals = lax.all_to_all(
        jnp.broadcast_to(total[None], (members, 1, 128)), everyone, 0, 0, tiled=True
    )
    clipped = scaled(place, totals, late, early, parcel, far, widths[0], entries)
    return (clipped[None], hidden_grad[None])


def solution(mesh):
    in_specs = (
        P("mod", ("loop", "line"), None),
        P("mod", ("loop", "line"), None),
        P("mod", None, None),
        P("mod", "loop", "line"),
    )
    out_specs = (P("mod", "loop", None), P("mod", ("loop", "line"), None))
    return jax.shard_map(
        on_device, mesh=mesh, in_specs=in_specs, out_specs=out_specs, check_vma=False
    )
```

```python
import functools

import jax
import jax.numpy as jnp
from jax import lax
from jax.experimental import pallas as pl
from jax.experimental.pallas import tpu as pltpu
from jax.sharding import PartitionSpec as P

CORES = 2
VMEM_BYTES = 12 * 2**20


def swap(x, axis, distance):
    size = lax.axis_size(axis)
    return lax.ppermute(x, axis, [(i, i ^ distance) for i in range(size)])


def doubled(size):
    distance = 1
    while distance < size:
        yield distance
        distance *= 2


def after(x, *ready):
    return lax.optimization_barrier((x, *ready))[0]


def piece(x, index):
    return lax.dynamic_index_in_dim(x, index, 0, keepdims=False)


def farthest_first(size):
    return sorted(range(1, size), key=lambda d: -(d ^ 1))


def parcels(x, index):
    return {d: piece(x, index[d]) for d in farthest_first(x.shape[0])}


def exchanged(sends, axis, stride=1):
    return [swap(x, axis, d * stride) for d, x in sends.items()]


def summed(own, parts):
    for part in parts:
        own = own + part
    return own


def product(left, right):
    return lax.dot_general(
        left, right, (((0,), (0,)), ((), ())), preferred_element_type=jnp.float32
    )


def first_kernel(start, count, place, act, dy, out, masked, tokens, columns, sems):
    width = columns.shape[1]
    half = dy.shape[1] // CORES
    column = pl.multiple_of((1 - place[0] % CORES) * half + start, 128)
    copies = [
        pltpu.make_async_copy(act, tokens, sems.at[0]),
        pltpu.make_async_copy(dy.at[:, pl.ds(column, width)], columns, sems.at[1]),
    ]
    for copy in copies:
        copy.start()
    copies[0].wait()
    live = lax.broadcasted_iota(jnp.int32, (act.shape[0], 1), 0) < count[0, 0, 0]
    masked[...] = jnp.where(live, tokens[...], jnp.zeros_like(tokens))
    copies[1].wait()
    out[...] = product(masked[...], columns[...])


def first_term(counts, place, act, dy, start, width):
    rows, hidden = act.shape
    smem = pl.BlockSpec(memory_space=pltpu.SMEM)
    vmem = pl.BlockSpec(memory_space=pltpu.VMEM)
    hbm = pl.BlockSpec(memory_space=pltpu.HBM)
    return pl.pallas_call(
        functools.partial(first_kernel, start),
        out_shape=(
            jax.ShapeDtypeStruct((hidden, width), jnp.float32),
            jax.ShapeDtypeStruct((rows, hidden), act.dtype),
        ),
        in_specs=[smem, smem, hbm, hbm],
        out_specs=(vmem,) * 2,
        scratch_shapes=[
            pltpu.VMEM((rows, hidden), act.dtype),
            pltpu.VMEM((rows, width), dy.dtype),
            pltpu.SemaphoreType.DMA((2,)),
        ],
        compiler_params=pltpu.CompilerParams(vmem_limit_bytes=VMEM_BYTES),
    )(
        counts,
        place,
        pltpu.with_memory_space_constraint(act, pltpu.HBM),
        pltpu.with_memory_space_constraint(dy, pltpu.HBM),
    )


def terms_kernel(spans, place, masked, dy, *outs):
    half = dy.shape[1] // CORES
    core = place[0] % CORES
    columns = []
    for (own, start), out in zip(spans, outs):
        column = pl.multiple_of((core if own else 1 - core) * half + start, 128)
        columns.append(dy[:, pl.ds(column, out.shape[1])])
    narrow = [i for i, out in enumerate(outs) if out.shape[1] <= 128]
    if len(narrow) == 2:
        both = product(masked[...], jnp.concatenate([columns[i] for i in narrow], axis=1))
        width = outs[narrow[0]].shape[1]
        outs[narrow[0]][...] = both[:, :width]
        outs[narrow[1]][...] = both[:, width:]
    for i, out in enumerate(outs):
        if len(narrow) != 2 or i not in narrow:
            out[...] = product(masked[...], columns[i])


def terms(place, masked, dy, *spans):
    vmem = pl.BlockSpec(memory_space=pltpu.VMEM)
    hidden = masked.shape[1]
    return pl.pallas_call(
        functools.partial(terms_kernel, [span[:2] for span in spans]),
        out_shape=tuple(jax.ShapeDtypeStruct((hidden, span[2]), jnp.float32) for span in spans),
        in_specs=[pl.BlockSpec(memory_space=pltpu.SMEM), vmem, vmem],
        out_specs=(vmem,) * len(spans),
        compiler_params=pltpu.CompilerParams(vmem_limit_bytes=VMEM_BYTES),
    )(place, masked, dy)


def scaled_kernel(entries, side, place, totals, late, early, parcel, *refs):
    *far, out, ordered = refs
    rows, block = out.shape
    half = block // CORES
    middle = late.shape[1]
    height, width = early.shape
    factor = 1.0 / jnp.sqrt(jnp.sum(totals[...]) / entries + 1e-06)
    pieces = [early[...], parcel[:, :width], *(x[...] for x in far)]
    for d, x in enumerate(pieces):
        ordered[place[0] ^ d] = x * factor
    for member in range(len(pieces)):
        row, column = member // CORES * height, member % CORES * half
        out[row : row + height, column : column + side] = ordered[member, :, :side]
        column += side + middle
        out[row : row + height, column : column + width - side] = ordered[member, :, side:]
    core = place[0] % CORES
    mine = pl.multiple_of(core * half + side, 128)
    other = pl.multiple_of((1 - core) * half + side, 128)
    out[:, pl.ds(mine, middle)] = late[...] * factor
    for part in range(rows // height):
        start = width + part * middle
        x = parcel[:, start : start + middle] * factor
        out[part * height : (part + 1) * height, pl.ds(other, middle)] = x


def scaled(place, totals, late, early, parcel, far, side, entries):
    smem = pl.BlockSpec(memory_space=pltpu.SMEM)
    vmem = pl.BlockSpec(memory_space=pltpu.VMEM)
    rows, middle = late.shape
    height, width = early.shape
    return pl.pallas_call(
        functools.partial(scaled_kernel, entries, side),
        out_shape=jax.ShapeDtypeStruct((rows, CORES * (width + middle)), jnp.float32),
        in_specs=[smem] + [vmem] * (4 + len(far)),
        out_specs=vmem,
        scratch_shapes=[pltpu.VMEM((CORES + len(far), height, width), jnp.float32)],
        compiler_params=pltpu.CompilerParams(vmem_limit_bytes=VMEM_BYTES),
    )(place, totals.reshape(-1, 128), late, early, parcel, *far)


def on_device(act, dy, w_out, counts):
    tokens = act[0]
    upstream = dy[0]
    weight = w_out[0]
    rows, hidden = tokens.shape
    block = weight.shape[1]
    n_loop = lax.axis_size("loop")
    n_y = lax.axis_size("line") // CORES
    z = lax.axis_index("loop").astype(jnp.uint32)
    line = lax.axis_index("line").astype(jnp.uint32)
    y = line // CORES
    place, low_y, over_z, over_y = lax.optimization_barrier(
        (
            line.astype(jnp.int32).reshape(1),
            y == 0,
            [z ^ d for d in range(n_loop)],
            [y ^ d for d in range(n_y)],
        )
    )
    own_rows = hidden // n_loop
    half = block // CORES
    tile = half // 5 // 128 * 128
    widths = (tile, 2 * tile, half - 3 * tile)

    live = lax.broadcasted_iota(jnp.int32, (rows, 1), 0) < counts[0, 0]
    entries = lax.axis_size("mod") * hidden * block

    def by_row_part(x):
        return x.reshape(n_loop, n_y, own_rows // n_y, -1).transpose(1, 0, 2, 3)

    side, middle, last = widths
    late_other, masked = first_term(counts, place, tokens, upstream, side, middle)
    late_other = swap(late_other, "line", 1)
    first_other, first_sum, late = terms(
        place, masked, upstream, (False, 0, side), (True, 0, side), (True, side, middle)
    )
    first_other = swap(first_other, "line", 1)
    second_other, second_sum = terms(
        place,
        masked,
        upstream,
        (False, side + middle, last),
        (True, side + middle, last),
    )
    second_other = swap(second_other, "line", 1)
    late = (late + late_other).reshape(n_loop, own_rows, widths[1])
    late_sends = parcels(late, over_z)
    farthest, *others = late_sends
    first_sum = by_row_part(first_sum + after(first_other, late_sends[farthest]))
    sends = parcels(first_sum, over_y)
    first_parts = exchanged(sends, "line", CORES)
    late_parts = exchanged(late_sends, "loop")
    second_sum = by_row_part(second_sum + after(second_other, *late_sends.values(), *sends.values()))
    sends = parcels(second_sum, over_y)
    second_parts = exchanged(sends, "line", CORES)
    first_parts = [after(part, *sends.values()) for part in first_parts]
    back = lax.dot_general(
        after(upstream, *sends.values()),
        weight,
        (((1,), (1,)), ((), ())),
        preferred_element_type=jnp.float32,
    )
    hidden_grad = jnp.where(live, back, jnp.zeros_like(back)).astype(jnp.bfloat16)

    early = jnp.concatenate(
        [
            summed(piece(x, over_y[0]), parts)
            for x, parts in ((first_sum, first_parts), (second_sum, second_parts))
        ],
        axis=-1,
    )
    sends = parcels(early, over_z)
    early_parts = exchanged(sends, "loop")
    late_parts = [after(part, *sends.values()) for part in late_parts]
    late = summed(piece(late, over_z[0]), late_parts)
    late = after(late, *sends.values())
    for d in doubled(n_y):
        late = late + swap(late, "line", d * CORES)
    early = summed(piece(early, over_z[0]), early_parts)

    squares = jnp.sum(early * early, axis=0).reshape(-1, 128).sum(0)
    squares_late = jnp.sum(late * late, axis=0).reshape(-1, 128).sum(0)
    total = (squares + jnp.where(low_y, squares_late, 0.0)).reshape(1, 128)
    total = after(total, hidden_grad)
    height = own_rows // n_y
    rows_late = [late[start : start + height] for start in range(0, own_rows, height)]
    parcel = jnp.concatenate([early, *rows_late], axis=1)
    far = [swap(after(early, parcel), "line", d) for d in range(CORES, n_y * CORES)]
    parcel = swap(parcel, "line", 1)
    everyone = ("mod", "loop", "line")
    members = lax.axis_size(everyone)
    totals = lax.all_to_all(
        jnp.broadcast_to(total[None], (members, 1, 128)), everyone, 0, 0, tiled=True
    )
    clipped = scaled(place, totals, late, early, parcel, far, widths[0], entries)
    return (clipped[None], hidden_grad[None])


def solution(mesh):
    in_specs = (
        P("mod", ("loop", "line"), None),
        P("mod", ("loop", "line"), None),
        P("mod", None, None),
        P("mod", "loop", "line"),
    )
    out_specs = (P("mod", "loop", None), P("mod", ("loop", "line"), None))
    return jax.shard_map(
        on_device, mesh=mesh, in_specs=in_specs, out_specs=out_specs, check_vma=False
    )
```
